32 devices in a mesh: rep: 4 (over z), fsdp: 8 (over y, x, core).
Axes of the slice: x: 2, y: 2, z: 4, core: 2. Of those that a mesh axis runs over, the one named last changes fastest.
Arguments:
- tokens: bfloat16 [32, 1024, 768], P(('rep', 'fsdp')), may hold values from -6 to 6
- segments: int32 [32, 1024], P(('rep', 'fsdp')), may hold values from 0 to 5, never falling along the last dimension, each value on 1 to 800 neighbouring positions
- w_in: bfloat16 [2, 768, 3328], P(None, 'fsdp'), may hold values from -0.21875 to 0.21875
- w_dt: bfloat16 [2, 768, 24], P(None, 'fsdp'), may hold values from -0.21875 to 0.21875
- w_out: bfloat16 [2, 1536, 768], P(None, 'fsdp'), may hold values from -0.15625 to 0.15625
- conv_w: bfloat16 [2, 4, 1792], P(None, None, 'fsdp'), may hold values from -3 to 3
- conv_b: bfloat16 [2, 1792], P(None, 'fsdp'), may hold values from -0.5 to 0.5
- norm_in: bfloat16 [2, 768], P(None, 'fsdp'), may hold values from 0.5 to 1.5
- norm_gate: bfloat16 [2, 1536], P(None, 'fsdp'), may hold values from 0.5 to 1.5
- dt_bias: float32 [2, 24], replicated, may hold values from -3 to -1
- a_log: float32 [2, 24], replicated, may hold values from -3 to 1.5
- d_skip: float32 [2, 24], replicated, may hold values from 0.5 to 1.5
- cotangent: bfloat16 [32, 1024, 768], P(('rep', 'fsdp')), may hold values from -6 to 6
Outputs:
- mixed: bfloat16 [32, 1024, 768], P(('rep', 'fsdp'))
- grad_tokens: float32 [32, 1024, 768], P(('rep', 'fsdp'))
- grad_w_in: float32 [2, 768, 3328], P(None, 'fsdp')
- grad_w_dt: float32 [2, 768, 24], P(None, 'fsdp')
- grad_w_out: float32 [2, 1536, 768], P(None, 'fsdp')
- grad_conv_w: float32 [2, 4, 1792], P(None, None, 'fsdp')
- grad_conv_b: float32 [2, 1792], P(None, 'fsdp')
- grad_norm_in: float32 [2, 768], P(None, 'fsdp')
- grad_norm_gate: float32 [2, 1536], P(None, 'fsdp')
- grad_dt_bias: float32 [2, 24], replicated
- grad_a_log: float32 [2, 24], replicated
- grad_d_skip: float32 [2, 24], replicated
The draws below stay inside these ranges and needn't reach their ends.
Inputs may be any that keep to these rules, and one draw needn't show every extreme that they name: `segments`: in each sequence the document numbers run from 0 to 5 without falling; each document has 1 to 800 tokens and one has exactly 800.
All inputs are finite; a program needn't handle non-finite values.
Results may differ from the reference program's by a relative error of at most 0.013.
Values may be sent and summed in bfloat16 or wider, within the bound.
A program may use at most 320 MiB of HBM per device.

```python
import math
import jax
import jax.numpy as jnp
import numpy as np
from jax import lax

D = 768
DI = 1536
CONV = 4
SPAN = 256
LAYERS = 2
LENGTH = 1024
H = 24
PROJ = 3328
XBC = 1792
DOCS = 6
DOC_MOST = 800
SEQS = 32


def block_scale(key, dims, cuts, least, top_value):
    def one(axis_at, blocks):
        steps = jax.random.uniform(jax.random.fold_in(jax.random.fold_in(key, 6), axis_at), (blocks,), jnp.float32, least / len(cuts), top_value / len(cuts))
        return jnp.repeat(jnp.exp(steps), dims[axis_at] // blocks).reshape((-1,) + (1,) * (len(dims) - axis_at - 1))

    factor_of = one(*cuts[0])
    for cut in cuts[1:]:
        factor_of = factor_of * one(*cut)
    return factor_of


def length_profile(amount, total, reach, slope):
    loads = [(1 << 20) // math.isqrt(standing ** slope) + 1 for standing in range(2, amount + 1)]
    surplus, counts = total - reach - (amount - 1), [1] * (amount - 1)
    while surplus > 0:
        free = [i for i in range(amount - 1) if counts[i] < reach]
        whole, remaining = sum([loads[i] for i in free]), surplus
        for i in free:
            addition = min(reach - counts[i], max(1, remaining * loads[i] // whole), surplus)
            counts[i] = counts[i] + addition
            surplus = surplus - addition
    return np.array([reach] + counts)


def ragged(own_key, number_of, total, most, slope):
    if number_of == 2:
        one = jax.random.randint(own_key, (), max(1, total - most), min(most, total - 1) + 1)
        return jnp.stack([one, total - one])
    lengths = jnp.asarray(length_profile(number_of, total, most, slope), jnp.int32)
    pairs = (number_of - 1) // 2
    giver, sink = lengths[1:1 + 2 * pairs:2], lengths[2:2 + 2 * pairs:2]
    margin = jnp.minimum(giver - 1, most - sink)
    moved = jax.random.randint(jax.random.fold_in(own_key, 1), (pairs,), 0, 1 << 20) % (margin + 1)
    lengths = lengths.at[1:1 + 2 * pairs:2].set(giver - moved).at[2:2 + 2 * pairs:2].set(sink + moved)
    return lengths[jax.random.permutation(jax.random.fold_in(own_key, 2), number_of)]


def gaussian(own_key, shape, deviation, most, split=(), kind=jnp.bfloat16):
    array = jax.random.normal(own_key, shape, jnp.float32) * deviation
    if len(split) > 0:
        array = block_scale(own_key, shape, split, -0.22, 0.18) * array
    return jnp.clip(array, min=-most, max=most).astype(kind)


def setup_inputs(seed: int = 0) -> dict:
    key_of = jax.random.split(jax.random.key(seed), 14)
    tokens = gaussian(key_of[0], (SEQS, LENGTH, D), 1.0, 6.0, ((0, 32),))
    segments = jax.vmap(lambda own: jnp.searchsorted(jnp.cumsum(ragged(own, DOCS, LENGTH, DOC_MOST, 2)), jnp.arange(LENGTH), side="right"))(jax.random.split(key_of[1], SEQS)).reshape((SEQS, LENGTH)).astype(jnp.int32)
    w_in = gaussian(key_of[2], (LAYERS, D, PROJ), D ** -0.5, 0.21875, ((1, 8),))
    w_dt = gaussian(key_of[3], (LAYERS, D, H), D ** -0.5, 0.21875, ((1, 8),))
    w_out = gaussian(key_of[4], (LAYERS, DI, D), DI ** -0.5, 0.15625, ((1, 8),))
    conv_w = gaussian(key_of[5], (LAYERS, CONV, XBC), CONV ** -0.5, 3.0, ((2, 8),))
    conv_b = jnp.clip(jax.random.uniform(key_of[6], (LAYERS, XBC), jnp.float32, -0.5, 0.5) * block_scale(key_of[6], (LAYERS, XBC), ((1, 8),), -0.4, 0.0), -0.5, 0.5).astype(jnp.bfloat16)
    norm_in = jnp.clip(1.0 + 0.1 * jax.random.normal(key_of[7], (LAYERS, D), jnp.float32), 0.5, 1.5).astype(jnp.bfloat16)
    norm_gate = jnp.clip(1.0 + 0.1 * jax.random.normal(key_of[8], (LAYERS, DI), jnp.float32), 0.5, 1.5).astype(jnp.bfloat16)
    dt_bias = jnp.clip(jax.random.uniform(key_of[9], (LAYERS, H), jnp.float32, -3.0, -1.0), -3.0, -1.0)
    a_log = jnp.clip(jax.random.uniform(key_of[10], (LAYERS, H), jnp.float32, -3.0, 1.5), -3.0, 1.5)
    d_skip = jnp.clip(jax.random.uniform(key_of[11], (LAYERS, H), jnp.float32, 0.5, 1.5), 0.5, 1.5)
    cotangent = gaussian(key_of[12], (SEQS, LENGTH, D), 1.0, 6.0, ((0, 32),))
    return {"tokens": tokens, "segments": segments, "w_in": w_in, "w_dt": w_dt, "w_out": w_out, "conv_w": conv_w, "conv_b": conv_b, "norm_in": norm_in, "norm_gate": norm_gate, "dt_bias": dt_bias, "a_log": a_log, "d_skip": d_skip, "cotangent": cotangent}


EPSILON = 1e-05
HIGHEST = lax.Precision.HIGHEST

@jax.custom_vjp
def low(v):
    return lax.optimization_barrier(v.astype(jnp.bfloat16)).astype(jnp.float32)

@jax.custom_vjp
def low_back(v):
    return v

def low_keep(v):
    return (low(v), None)

def low_pass(kept, grad):
    return (grad,)

def back_keep(v):
    return (v, None)

def back_low(kept, grad):
    return (low(grad),)
low.defvjp(low_keep, low_pass)
low_back.defvjp(back_keep, back_low)

def normalize(values, weight):
    return values * lax.rsqrt(lax.optimization_barrier(jnp.mean(values * values, axis=-1, keepdims=True)) + EPSILON) * weight

def block_step(carry_state, inputs):
    values_block, b_block, c_block, dt_block, rate_block, seg_block, carried_block = inputs
    cumulative = jnp.cumsum(rate_block, axis=0)
    position = jnp.arange(seg_block.shape[0])
    lower_tri = position[:, None] >= position[None, :]
    same_doc = (lower_tri & (seg_block[:, None] == seg_block[None, :])).astype(rate_block.dtype)
    by_head = cumulative.T
    log_decay = by_head[:, :, None] - by_head[:, None, :]
    decay_mat = jnp.exp(jnp.where(same_doc[None] > 0, log_decay, 0.0)) * same_doc[None]
    intersection = jnp.dot(c_block, b_block.T, precision=HIGHEST)
    mixing = decay_mat * intersection[None] * dt_block.T[:, None, :]
    inside = jnp.einsum('hij,jhp->ihp', mixing, values_block, precision=HIGHEST)
    outside = jnp.einsum('in,hpn->ihp', c_block, carry_state, precision=HIGHEST)
    outside = outside * (carried_block[:, None] * jnp.exp(cumulative))[:, :, None]
    last_rate = cumulative[-1]
    weight_last = jnp.exp(last_rate[None, :] - cumulative) * (seg_block == seg_block[-1]).astype(rate_block.dtype)[:, None] * dt_block
    new_state = carry_state * (carried_block[-1] * jnp.exp(last_rate))[:, None, None]
    new_state = new_state + jnp.einsum('jh,jhp,jn->hpn', weight_last, values_block, b_block, precision=HIGHEST)
    return (new_state, inside + outside)

def mixer(projected, dt_raw, segment, conv_weight, conv_bias, gate_gain, bias_dt, log_rate, skip_gain):
    length = projected.shape[0]
    inner = gate_gain.shape[0]
    heads = bias_dt.shape[0]
    headdim = inner // heads
    state_size = (projected.shape[1] - 2 * inner) // 2
    kernel = conv_weight.shape[0]
    gate_part = projected[:, :inner]
    conv_in = projected[:, inner:]
    summed = conv_bias[None, :] + conv_weight[kernel - 1][None, :] * conv_in
    for shift_by in range(1, kernel):
        shifted = jnp.pad(conv_in, ((shift_by, 0), (0, 0)))[:length]
        shifted_seg = jnp.pad(segment, (shift_by, 0), constant_values=-1)[:length]
        keeping = (shifted_seg == segment).astype(projected.dtype)
        summed = summed + conv_weight[kernel - 1 - shift_by][None, :] * shifted * keeping[:, None]
    conv_out = jax.nn.silu(summed)
    values = conv_out[:, :inner].reshape(length, heads, headdim)
    b_input = conv_out[:, inner:inner + state_size]
    c_output = conv_out[:, inner + state_size:]
    step_dt = jax.nn.softplus(dt_raw + bias_dt[None, :])
    decay_rate = -jnp.exp(log_rate)[None, :] * step_dt
    blocks = length // SPAN
    seg_blocks = segment.reshape(blocks, SPAN)
    before = jnp.concatenate([jnp.full((1,), -1, jnp.int32), seg_blocks[:-1, -1].astype(jnp.int32)])
    carried = (seg_blocks == before[:, None]).astype(projected.dtype)
    scanned = (values.reshape(blocks, SPAN, heads, headdim), b_input.reshape(blocks, SPAN, state_size), c_output.reshape(blocks, SPAN, state_size), step_dt.reshape(blocks, SPAN, heads), decay_rate.reshape(blocks, SPAN, heads), seg_blocks, carried)
    initial = jnp.zeros((heads, headdim, state_size), projected.dtype)
    unused, outputs = lax.scan(jax.checkpoint(block_step), initial, scanned)
    result = outputs.reshape(length, heads, headdim) + skip_gain[None, :, None] * values
    result = result.reshape(length, inner) * jax.nn.silu(gate_part)
    return normalize(result, gate_gain[None, :])

def forward_layers(hidden, params, segment):
    in_weights, dt_weights, out_weights, conv_weight, conv_bias, norm_gain, gate_gain, bias_dt, log_rate, skip_gain = params
    for layer_index in range(LAYERS):
        normed = low(normalize(hidden, norm_gain[layer_index]))
        projected = low_back(jnp.einsum('gld,dp->glp', normed, in_weights[layer_index], precision=HIGHEST))
        dt_raw = low_back(jnp.einsum('gld,dp->glp', normed, dt_weights[layer_index], precision=HIGHEST))
        gated = jax.vmap(mixer, in_axes=(0, 0, 0, None, None, None, None, None, None))(projected, dt_raw, segment, conv_weight[layer_index], conv_bias[layer_index], gate_gain[layer_index], bias_dt[layer_index], log_rate[layer_index], skip_gain[layer_index])
        branch = low_back(jnp.einsum('gli,id->gld', low(gated), out_weights[layer_index], precision=HIGHEST))
        hidden = hidden + branch
    return hidden

def reference(tokens, segments, w_in, w_dt, w_out, conv_w, conv_b, norm_in, norm_gate, dt_bias, a_log, d_skip, cotangent):
    params = tuple((member.astype(jnp.float32) for member in (w_in, w_dt, w_out, conv_w, conv_b, norm_in, norm_gate, dt_bias, a_log, d_skip)))
    group_size = 4 if SEQS % 4 == 0 else 1
    group_count = SEQS // group_size
    token_groups = tokens.astype(jnp.float32).reshape(group_count, group_size, LENGTH, D)
    seg_groups = segments.reshape(group_count, group_size, LENGTH)
    cot_groups = cotangent.astype(jnp.float32).reshape(group_count, group_size, LENGTH, D)

    def one_group(totals, items):
        tok_group, seg_group, cot_group = items

        def run_layers(hidden, weights):
            return forward_layers(hidden, weights, seg_group)
        result, back_fn = jax.vjp(run_layers, tok_group, params)
        grad_hidden, grad_params = back_fn(cot_group)
        totals = jax.tree.map(lambda left, right: left + right, totals, grad_params)
        return (totals, (result.astype(jnp.bfloat16), grad_hidden))
    initial = jax.tree.map(jnp.zeros_like, params)
    totals, (mixed_all, grad_all) = lax.scan(one_group, initial, (token_groups, seg_groups, cot_groups))
    return (mixed_all.reshape(SEQS, LENGTH, D), grad_all.reshape(SEQS, LENGTH, D), totals[0], totals[1], totals[2], totals[3], totals[4], totals[5], totals[6], totals[7], totals[8], totals[9])
```

```python
import functools

import jax
import jax.numpy as jnp
from jax import lax
from jax.experimental import pallas as pl
from jax.experimental.pallas import tpu as pltpu
from jax.sharding import PartitionSpec as P

EPSILON = 1e-05
ROWS = 256
CHUNK = 128
LANES = 128
HALO = 8
HIGHEST = lax.Precision.HIGHEST
F32 = jnp.float32
BF16 = jnp.bfloat16
VMEM_BYTES = 56 * 1024 * 1024


def dot_nn(left, right, precision=None):
    return lax.dot_general(
        left, right, (((1,), (0,)), ((), ())), preferred_element_type=F32, precision=precision
    )


def dot_nt(left, right):
    return lax.dot_general(left, right, (((1,), (1,)), ((), ())), preferred_element_type=F32)


def dot_tn(left, right):
    return lax.dot_general(left, right, (((0,), (0,)), ((), ())), preferred_element_type=F32)


def sigmoid(v):
    return 0.5 * jnp.tanh(0.5 * v) + 0.5


def softplus(v):
    return jnp.maximum(v, 0.0) + jnp.log1p(jnp.exp(-jnp.abs(v)))


def iota2(shape, axis):
    return lax.broadcasted_iota(jnp.int32, shape, axis)


def column(values, index):
    return values[:, index : index + 1]


def spread(values, pair, low_half):
    return jnp.where(low_half, column(values, 2 * pair), column(values, 2 * pair + 1))


def convolve(ext_ref, taps_ref, bias_ref, masks, at):
    rows = masks.shape[0]
    cols = pl.ds(at, LANES)
    total = bias_ref[:, cols] + taps_ref[3:4, cols] * ext_ref[HALO : HALO + rows, cols]
    for back in range(1, 4):
        shifted = ext_ref[HALO - back : HALO - back + rows, cols]
        total = total + taps_ref[3 - back : 4 - back, cols] * shifted * column(masks, back - 1)
    return total


def forward_kernel(
    sizes,
    h_ref, masks_ref, segr_ref, w_ref, wout_ref, taps_ref, cbias_ref, gin_ref, ggate_ref,
    head_ref, skip_ref,
    next_ref, normed_ref, proj_ref, y_ref, gated_ref, states_ref,
    ext, xs, state,
):
    inner, xbc, nstate, pairs = sizes
    rows = h_ref.shape[0]

    @pl.when(pl.program_id(0) == 0)
    def _():
        state[...] = jnp.zeros_like(state)
        ext[0:HALO, :] = jnp.zeros((HALO, xbc), F32)

    hidden = h_ref[...].astype(F32)
    scale = lax.rsqrt(jnp.mean(hidden * hidden, axis=-1, keepdims=True) + EPSILON)
    normed_ref[...] = (hidden * scale * gin_ref[...]).astype(BF16)
    proj_ref[...] = dot_nn(normed_ref[...], w_ref[...])
    masks = masks_ref[...]
    ext[HALO : HALO + rows, :] = proj_ref[:, inner : inner + xbc]
    for at in range(0, xbc, LANES):
        v = convolve(ext, taps_ref, cbias_ref, masks, at)
        xs[:, at : at + LANES] = v * sigmoid(v)
    ext[0:HALO, :] = ext[rows : rows + HALO, :]

    low_half = iota2((CHUNK, LANES), 1) < LANES // 2
    low_row = iota2((1, LANES), 1) < LANES // 2
    t_at, s_at = iota2((CHUNK, CHUNK), 0), iota2((CHUNK, CHUNK), 1)
    tri = (t_at >= s_at).astype(F32)

    @pl.loop(0, rows // CHUNK)
    def _(c):
        span = pl.ds(pl.multiple_of(c * CHUNK, CHUNK), CHUNK)
        mk = masks_ref[span, :]
        dt = softplus(proj_ref[span, inner + xbc : inner + xbc + LANES] + head_ref[0:1, :])
        cum = dot_nn(tri, -head_ref[1:2, :] * dt, HIGHEST)
        cum_t, dt_t = cum.T, dt.T
        segr = segr_ref[c]
        bias = jnp.where((t_at >= s_at) & (column(mk, 8) == segr), 0.0, -1e30)
        b_f = xs[span, inner : inner + nstate]
        c_b = xs[span, inner + nstate : inner + 2 * nstate].astype(BF16)
        both = dot_nt(c_b, b_f.astype(BF16))
        b_t = b_f.T.astype(BF16)
        last = cum[CHUNK - 1 : CHUNK, :]
        from_state = jnp.exp(cum) * column(mk, 3)
        to_state = jnp.exp(last - cum) * column(mk, 4) * dt
        keep = jnp.exp(last) * mk[CHUNK - 1 : CHUNK, 3:4]
        for pair in range(pairs):
            cols = pl.ds(pair * LANES, LANES)
            x = xs[span, cols]
            x_b = x.astype(BF16)
            parts = []
            for head in (2 * pair, 2 * pair + 1):
                decay = jnp.exp(column(cum, head) - cum_t[head : head + 1, :] + bias)
                mix = decay * both * dt_t[head : head + 1, :]
                parts.append(dot_nn(mix.astype(BF16), x_b))
            inside = jnp.where(low_half, parts[0], parts[1])
            old = state[:, cols]
            states_ref[c, :, cols] = old
            outside = dot_nn(c_b, old.astype(BF16)) * spread(from_state, pair, low_half)
            fresh = dot_nn(b_t, (x * spread(to_state, pair, low_half)).astype(BF16))
            state[:, cols] = old * spread(keep, pair, low_row) + fresh
            y_ref[span, cols] = inside + outside + skip_ref[:, cols] * x

    total = jnp.zeros((rows, LANES), F32)
    for at in range(0, inner, LANES):
        z = proj_ref[:, at : at + LANES]
        g = y_ref[:, at : at + LANES] * (z * sigmoid(z))
        xs[:, at : at + LANES] = g
        total = total + g * g
    scale = lax.rsqrt(jnp.sum(total, axis=-1, keepdims=True) / inner + EPSILON)
    for at in range(0, inner, LANES):
        g = xs[:, at : at + LANES] * scale * ggate_ref[:, at : at + LANES]
        gated_ref[:, at : at + LANES] = g.astype(BF16)
    out = h_ref[...].astype(F32) + dot_nn(gated_ref[...], wout_ref[...])
    next_ref[...] = out.astype(next_ref.dtype)


def backward_kernel(
    sizes,
    dh_ref, h_ref, masks_ref, segr_ref, proj_ref, before_ref, y_ref, states_ref,
    w_ref, wout_ref, taps_ref, cbias_ref, gin_ref, ggate_ref, head_ref, skip_ref, fold_ref,
    dnext_ref, dproj_ref, sg_gate, sg_conv, sg_in, sg_skip, sg_head,
    ext, xs, conv, dy, dxs, dstate, rowsc, flat,
):
    inner, xbc, nstate, pairs = sizes
    rows = h_ref.shape[0]
    step = pl.program_id(0)

    @pl.when(step == 0)
    def _():
        dstate[...] = jnp.zeros_like(dstate)
        rowsc[...] = jnp.zeros_like(rowsc)
        flat[...] = jnp.zeros_like(flat)
        dxs[rows : rows + HALO, :] = jnp.zeros((HALO, xbc), F32)
        for ref in (sg_gate, sg_conv, sg_in, sg_skip, sg_head):
            ref[...] = jnp.zeros_like(ref)

    dh = dh_ref[...].astype(F32)
    dy[...] = dot_nt(dh.astype(BF16), wout_ref[...])

    squares = jnp.zeros((rows, LANES), F32)
    cross = jnp.zeros((rows, LANES), F32)
    for at in range(0, inner, LANES):
        cols = pl.ds(at, LANES)
        z = proj_ref[:, cols]
        g = y_ref[:, cols] * (z * sigmoid(z))
        squares = squares + g * g
        cross = cross + g * (dy[:, cols] * ggate_ref[:, cols])
    scale = lax.rsqrt(jnp.sum(squares, axis=-1, keepdims=True) / inner + EPSILON)
    mean = scale * jnp.sum(cross, axis=-1, keepdims=True) / inner
    for at in range(0, inner, LANES):
        cols = pl.ds(at, LANES)
        z = proj_ref[:, cols]
        sig = sigmoid(z)
        gate = z * sig
        y = y_ref[:, cols]
        m = y * gate * scale
        dgated = dy[:, cols]
        sg_gate[0:1, cols] += jnp.sum(m * dgated, axis=0, keepdims=True)
        dg = scale * (dgated * ggate_ref[:, cols] - m * mean)
        dproj_ref[:, cols] = (dg * y * (sig * (1.0 + z * (1.0 - sig)))).astype(BF16)
        dy[:, cols] = dg * gate

    masks = masks_ref[...]
    ext[0:HALO, :] = before_ref[:, inner : inner + xbc]
    ext[HALO : HALO + rows, :] = proj_ref[:, inner : inner + xbc]
    for at in range(0, xbc, LANES):
        v = convolve(ext, taps_ref, cbias_ref, masks, at)
        conv[:, at : at + LANES] = v
        xs[:, at : at + LANES] = v * sigmoid(v)

    low_half = iota2((CHUNK, LANES), 1) < LANES // 2
    low_row = iota2((1, LANES), 1) < LANES // 2
    lane = iota2((CHUNK, LANES), 1)
    s_at, t_at = iota2((CHUNK, CHUNK), 0), iota2((CHUNK, CHUNK), 1)
    tri = (s_at >= t_at).astype(F32)
    tri_t = (s_at <= t_at).astype(F32)
    last_row = iota2((CHUNK, LANES), 0) == CHUNK - 1
    chunks = rows // CHUNK

    @pl.loop(0, chunks)
    def _(back):
        c = chunks - 1 - back
        span = pl.ds(pl.multiple_of(c * CHUNK, CHUNK), CHUNK)
        mk = masks_ref[span, :]
        raw = proj_ref[span, inner + xbc : inner + xbc + LANES] + head_ref[0:1, :]
        dt = softplus(raw)
        speed = head_ref[1:2, :]
        cum = dot_nn(tri, -speed * dt, HIGHEST)
        cum_t = cum.T
        segr = segr_ref[c]
        bias = jnp.where((s_at <= t_at) & (column(mk, 8) == segr), 0.0, -1e30)
        b_b = xs[span, inner : inner + nstate].astype(BF16)
        c_f = xs[span, inner + nstate : inner + 2 * nstate]
        c_b = c_f.astype(BF16)
        c_t = c_f.T.astype(BF16)
        both = dot_nt(b_b, c_b)
        last = cum[CHUNK - 1 : CHUNK, :]
        from_state = jnp.exp(cum) * column(mk, 3)
        to_bare = jnp.exp(last - cum) * column(mk, 4)
        to_state = to_bare * dt
        keep = jnp.exp(last) * mk[CHUNK - 1 : CHUNK, 3:4]
        dboth = jnp.zeros((CHUNK, CHUNK), F32)
        db = jnp.zeros((CHUNK, nstate), F32)
        dc = jnp.zeros((CHUNK, nstate), F32)
        ddt = jnp.zeros((CHUNK, LANES), F32)
        dto = jnp.zeros((CHUNK, LANES), F32)
        dfrom = jnp.zeros((CHUNK, LANES), F32)
        for pair in range(pairs):
            cols = pl.ds(pair * LANES, LANES)
            x = xs[span, cols]
            d = dy[span, cols]
            d_b = d.astype(BF16)
            old = states_ref[c, :, cols]
            old_b = old.astype(BF16)
            dnew = dstate[:, cols]
            dnew_b = dnew.astype(BF16)
            weight = spread(to_state, pair, low_half)
            scaled = d * spread(from_state, pair, low_half)
            scaled_b = scaled.astype(BF16)
            reach = scaled * dot_nn(c_b, old_b)
            pull = dot_nn(b_b, dnew_b)
            dc = dc + dot_nt(scaled_b, old_b)
            db = db + dot_nt((x * weight).astype(BF16), dnew_b)
            flat[0:1, cols] = jnp.sum(dnew * old, axis=0, keepdims=True)
            dstate[:, cols] = dot_nn(c_t, scaled_b) + dnew * spread(keep, pair, low_row)
            gain = x * pull
            parts = []
            for head in (2 * pair, 2 * pair + 1):
                mine = low_half if head % 2 == 0 else jnp.logical_not(low_half)
                dt_col = column(dt, head)
                x_m = jnp.where(mine, x, 0.0).astype(BF16)
                decay = jnp.exp(cum_t[head : head + 1, :] - column(cum, head) + bias)
                prod = dot_nt(x_m, d_b)
                mix = decay * both
                parts.append(dot_nn(mix.astype(BF16), d_b))
                inner_prod = mix * prod
                dboth = dboth + decay * prod * dt_col
                rowsc[head : head + 1, :] = jnp.sum(inner_prod * dt_col, axis=0, keepdims=True)
                here = lane == head
                ddt = jnp.where(here, jnp.sum(inner_prod, axis=1, keepdims=True), ddt)
                dto = jnp.where(
                    here, jnp.sum(jnp.where(mine, gain, 0.0), axis=1, keepdims=True), dto
                )
                dfrom = jnp.where(
                    here, jnp.sum(jnp.where(mine, reach, 0.0), axis=1, keepdims=True), dfrom
                )
            inside = jnp.where(low_half, parts[0], parts[1]) * spread(dt, pair, low_half)
            dxs[span, cols] = inside + weight * pull + skip_ref[:, cols] * d
            sg_skip[0:1, cols] += jnp.sum(d * x, axis=0, keepdims=True)
        dxs[span, inner : inner + nstate] = db + dot_nn(dboth.astype(BF16), c_b)
        dxs[span, inner + nstate : inner + 2 * nstate] = dc + dot_nn(dboth.T.astype(BF16), b_b)
        moved = dto * to_state
        dlast = dot_nn(flat[...], fold_ref[...], HIGHEST)[0:1, :] * keep
        dlast = dlast + jnp.sum(moved, axis=0, keepdims=True)
        dcum = rowsc[...].T + dfrom - dt * ddt - moved
        dcum = dcum + jnp.where(last_row, dlast, 0.0)
        drate = dot_nn(tri_t, dcum, HIGHEST)
        dtotal = ddt + dto * to_bare - speed * drate
        draw = dtotal * sigmoid(raw)
        dproj_ref[span, inner + xbc : inner + xbc + LANES] = draw.astype(BF16)
        sg_head[0:1, :] += jnp.sum(draw, axis=0, keepdims=True)
        sg_head[1:2, :] += jnp.sum(-speed * dt * drate, axis=0, keepdims=True)

    for at in range(0, xbc, LANES):
        cols = pl.ds(at, LANES)
        v = conv[:, cols]
        sig = sigmoid(v)
        dconv = dxs[0:rows, cols] * (sig * (1.0 + v * (1.0 - sig)))
        dxs[0:rows, cols] = dconv
        sg_conv[4:5, cols] += jnp.sum(dconv, axis=0, keepdims=True)
        sg_conv[3:4, cols] += jnp.sum(dconv * ext[HALO : HALO + rows, cols], axis=0, keepdims=True)
        total = dconv * taps_ref[3:4, cols]
        for back in range(1, 4):
            shifted = ext[HALO - back : HALO - back + rows, cols] * column(masks, back - 1)
            sg_conv[3 - back : 4 - back, cols] += jnp.sum(dconv * shifted, axis=0, keepdims=True)
            later = dxs[back : back + rows, cols] * column(masks, 4 + back)
            total = total + later * taps_ref[3 - back : 4 - back, cols]
        dproj_ref[:, inner + at : inner + at + LANES] = total.astype(BF16)
    dxs[rows : rows + HALO, :] = dxs[0:HALO, :]

    dnormed = dot_nt(dproj_ref[...], w_ref[...])
    hidden = h_ref[...].astype(F32)
    scale = lax.rsqrt(jnp.mean(hidden * hidden, axis=-1, keepdims=True) + EPSILON)
    m = hidden * scale
    sg_in[0:1, :] += jnp.sum(m * dnormed, axis=0, keepdims=True)
    dm = dnormed * gin_ref[...]
    dnext_ref[...] = dh_ref[...].astype(F32) + scale * (
        dm - m * jnp.mean(dm * m, axis=-1, keepdims=True)
    )


def whole(array):
    return pl.BlockSpec(array.shape, lambda i: (0,) * array.ndim)


def dims(hidden, weights):
    length, width = hidden.shape
    inner = weights["w_out"].shape[0]
    xbc = weights["taps"].shape[1]
    nstate = (xbc - inner) // 2
    return length, width, inner, xbc, nstate, inner // LANES


def run_forward(hidden, masks, segr, weights, heads, skip, out_type):
    length, width, inner, xbc, nstate, pairs = dims(hidden, weights)
    packed = inner + xbc + LANES
    steps = length // ROWS
    per = ROWS // CHUNK

    def rows(cols):
        return pl.BlockSpec((ROWS, cols), lambda i: (i, 0))

    fixed = (weights["w"], weights["w_out"], weights["taps"], weights["cbias"], weights["g_in"],
             weights["g_gate"], heads, skip)
    return pl.pallas_call(
        functools.partial(forward_kernel, (inner, xbc, nstate, pairs)),
        grid=(steps,),
        in_specs=[rows(width), rows(masks.shape[1]),
                  pl.BlockSpec((per, 1, CHUNK), lambda i: (i, 0, 0))] + [whole(a) for a in fixed],
        out_specs=[rows(width), rows(width), rows(packed), rows(inner), rows(inner),
                   pl.BlockSpec((per, nstate, inner), lambda i: (i, 0, 0))],
        out_shape=[
            jax.ShapeDtypeStruct((length, width), out_type),
            jax.ShapeDtypeStruct((length, width), BF16),
            jax.ShapeDtypeStruct((length, packed), F32),
            jax.ShapeDtypeStruct((length, inner), F32),
            jax.ShapeDtypeStruct((length, inner), BF16),
            jax.ShapeDtypeStruct((length // CHUNK, nstate, inner), F32),
        ],
        scratch_shapes=[
            pltpu.VMEM((ROWS + HALO, xbc), F32),
            pltpu.VMEM((ROWS, xbc), F32),
            pltpu.VMEM((nstate, inner), F32),
        ],
        compiler_params=pltpu.CompilerParams(vmem_limit_bytes=VMEM_BYTES),
        cost_estimate=pl.CostEstimate(
            flops=60_000_000_000, bytes_accessed=60_000_000, transcendentals=6_000_000),
        name="layer_forward",
    )(hidden, masks, segr, *fixed)


def run_backward(grad, hidden, masks, segr, saved, weights, heads, skip, fold):
    length, width, inner, xbc, nstate, pairs = dims(hidden, weights)
    packed = inner + xbc + LANES
    steps = length // ROWS
    per = ROWS // CHUNK
    proj, y, states = saved

    def rows(cols):
        return pl.BlockSpec((ROWS, cols), lambda i: (steps - 1 - i, 0))

    def before(i):
        return (jnp.maximum((steps - 1 - i) * (ROWS // HALO) - 1, 0), 0)

    fixed = (weights["w"], weights["w_out"], weights["taps"], weights["cbias"], weights["g_in"],
             weights["g_gate"], heads, skip, fold)
    sums = [(8, inner), (8, xbc), (8, width), (8, inner), (8, LANES)]
    return pl.pallas_call(
        functools.partial(backward_kernel, (inner, xbc, nstate, pairs)),
        grid=(steps,),
        in_specs=[rows(width), rows(width), rows(masks.shape[1]),
                  pl.BlockSpec((per, 1, CHUNK), lambda i: (steps - 1 - i, 0, 0)),
                  rows(packed), pl.BlockSpec((HALO, packed), before), rows(inner),
                  pl.BlockSpec((per, nstate, inner), lambda i: (steps - 1 - i, 0, 0))]
        + [pl.BlockSpec(a.shape, lambda i: (0, 0), pipeline_mode=pl.Buffered(1)) for a in fixed],
        out_specs=[rows(width), rows(packed)] + [pl.BlockSpec(s, lambda i: (0, 0)) for s in sums],
        out_shape=[
            jax.ShapeDtypeStruct((length, width), F32),
            jax.ShapeDtypeStruct((length, packed), BF16),
        ] + [jax.ShapeDtypeStruct(s, F32) for s in sums],
        scratch_shapes=[
            pltpu.VMEM((ROWS + HALO, xbc), F32),
            pltpu.VMEM((ROWS, xbc), F32),
            pltpu.VMEM((ROWS, xbc), F32),
            pltpu.VMEM((ROWS, inner), F32),
            pltpu.VMEM((ROWS + HALO, xbc), F32),
            pltpu.VMEM((nstate, inner), F32),
            pltpu.VMEM((LANES, CHUNK), F32),
            pltpu.VMEM((8, inner), F32),
        ],
        compiler_params=pltpu.CompilerParams(vmem_limit_bytes=VMEM_BYTES),
        cost_estimate=pl.CostEstimate(
            flops=120_000_000_000, bytes_accessed=80_000_000, transcendentals=6_000_000),
        name="layer_backward",
    )(grad, hidden, masks, segr, proj, proj, y, states, *fixed)


def token_masks(segment):
    length = segment.shape[0]
    blocks = segment.reshape(length // CHUNK, CHUNK)
    keeps, laters = [], []
    for back in range(1, 4):
        same = (segment[back:] == segment[:-back]).astype(F32)
        keeps.append(jnp.pad(same, (back, 0)))
        laters.append(jnp.pad(same, (0, back)))
    before = jnp.concatenate([jnp.full((1,), -1, jnp.int32), blocks[:-1, -1]])
    carried = (blocks == before[:, None]).astype(F32).reshape(length)
    lasting = (blocks == blocks[:, -1:]).astype(F32).reshape(length)
    number = segment.astype(F32)
    columns = keeps + [carried, lasting] + laters + [number]
    masks = jnp.pad(jnp.stack(columns, axis=1), ((0, 0), (0, 16 - len(columns))))
    return masks, number.reshape(length // CHUNK, 1, CHUNK)


def gather_layer(w_in, w_dt, w_out, conv_w, conv_b, norm_in, norm_gate, heads):
    wide = jnp.concatenate([w_in, jnp.pad(w_dt, ((0, 0), (0, LANES - heads)))], axis=1)
    small = jnp.concatenate([conv_w.reshape(-1), conv_b, norm_in, norm_gate])
    taps, chan, gain_in, gain_gate = conv_w.shape[0], conv_b.shape[0], norm_in.size, norm_gate.size
    wide = lax.all_gather(wide, "fsdp", axis=0, tiled=True)
    w_out = lax.all_gather(w_out, "fsdp", axis=0, tiled=True)
    small = lax.all_gather(small, "fsdp", axis=0).astype(F32)
    cut = taps * chan
    conv = small[:, :cut].reshape(-1, taps, chan).transpose(1, 0, 2).reshape(taps, -1)
    return {
        "w": wide,
        "w_out": w_out,
        "taps": jnp.pad(conv, ((0, 8 - taps), (0, 0))),
        "cbias": small[:, cut : cut + chan].reshape(1, -1),
        "g_in": small[:, cut + chan : cut + chan + gain_in].reshape(1, -1),
        "g_gate": small[:, cut + chan + gain_in :].reshape(1, -1),
    }


def owned_sum(values):
    part = lax.psum_scatter(values.astype(BF16), "fsdp", scatter_dimension=0, tiled=True)
    return lax.psum(part, "rep").astype(F32)


def shards(
    tokens, segments, w_in, w_dt, w_out, conv_w, conv_b, norm_in, norm_gate,
    dt_bias, a_log, d_skip, cotangent,
):
    layers, heads = dt_bias.shape
    group = lax.axis_size("fsdp")
    masks, segr = token_masks(segments[0])
    headdim = w_out.shape[1] * group // heads
    inner = heads * headdim
    fold = (jnp.arange(inner)[:, None] // headdim == jnp.arange(LANES)[None, :]).astype(F32)
    weights, head_rows, skips = [], [], []
    for l in range(layers):
        weights.append(gather_layer(
            w_in[l], w_dt[l], w_out[l], conv_w[l], conv_b[l], norm_in[l], norm_gate[l], heads))
        both = jnp.stack([dt_bias[l], jnp.exp(a_log[l])])
        head_rows.append(jnp.pad(both, ((0, 6), (0, LANES - heads))))
        skips.append(jnp.repeat(d_skip[l], headdim)[None, :])
    hiddens, saved = [tokens[0]], []
    for l in range(layers):
        out_type = BF16 if l == layers - 1 else F32
        following, normed, proj, y, gated, states = run_forward(
            hiddens[l], masks, segr, weights[l], head_rows[l], skips[l], out_type)
        hiddens.append(following)
        saved.append((normed, gated, (proj, y, states)))
    grad = cotangent[0]
    wide, outs, smalls, per_head = [None] * layers, [None] * layers, [None] * layers, [None] * layers
    for l in reversed(range(layers)):
        normed, gated, kept = saved[l]
        outs[l] = owned_sum(dot_tn(gated, grad.astype(BF16)))
        grad, dproj, s_gate, s_conv, s_in, s_skip, s_head = run_backward(
            grad, hiddens[l], masks, segr, kept, weights[l], head_rows[l], skips[l], fold)
        wide[l] = owned_sum(dot_tn(normed, dproj))
        smalls[l] = jnp.concatenate([
            s_conv[:5].reshape(5, group, -1).transpose(1, 0, 2).reshape(group, -1),
            s_in[0].reshape(group, -1),
            s_gate[0].reshape(group, -1),
        ], axis=1)
        per_head[l] = jnp.stack([
            s_head[0, :heads], s_head[1, :heads], s_skip[0].reshape(heads, headdim).sum(-1)])
    small = jnp.stack(smalls, axis=1)
    small = lax.psum_scatter(small, "fsdp", scatter_dimension=0, tiled=True)[0]
    small = lax.psum(small, "rep")
    chan, gain = conv_b.shape[1], norm_in.shape[1]
    columns = w_in.shape[2]
    head_sums = lax.psum(jnp.stack(per_head, axis=1), ("rep", "fsdp"))
    wide = jnp.stack(wide)
    return (
        hiddens[-1][None],
        grad[None],
        wide[:, :, :columns],
        wide[:, :, columns : columns + heads],
        jnp.stack(outs),
        small[:, : 4 * chan].reshape(layers, 4, chan),
        small[:, 4 * chan : 5 * chan],
        small[:, 5 * chan : 5 * chan + gain],
        small[:, 5 * chan + gain :],
        head_sums[0],
        head_sums[1],
        head_sums[2],
    )


def solution(mesh):
    sharded = P(None, "fsdp", None)
    tokens = P(("rep", "fsdp"), None, None)
    narrow = P(None, "fsdp")
    return jax.shard_map(
        shards,
        mesh=mesh,
        in_specs=(
            tokens, P(("rep", "fsdp"), None), sharded, sharded, sharded, P(None, None, "fsdp"),
            narrow, narrow, narrow, P(), P(), P(), tokens,
        ),
        out_specs=(
            tokens, tokens, sharded, sharded, sharded, P(None, None, "fsdp"),
            narrow, narrow, narrow, P(), P(), P(),
        ),
        check_vma=False,
    )
```

```python
import functools

import jax
import jax.numpy as jnp
from jax import lax
from jax.experimental import pallas as pl
from jax.experimental.pallas import tpu as pltpu
from jax.sharding import PartitionSpec as P

EPSILON = 1e-05
ROWS = 256
CHUNK = 128
LANES = 128
HALO = 8
HIGHEST = lax.Precision.HIGHEST
F32 = jnp.float32
BF16 = jnp.bfloat16
VMEM_BYTES = 56 * 1024 * 1024


def dot_nn(left, right, precision=None):
    return lax.dot_general(
        left, right, (((1,), (0,)), ((), ())), preferred_element_type=F32, precision=precision
    )


def dot_nt(left, right):
    return lax.dot_general(left, right, (((1,), (1,)), ((), ())), preferred_element_type=F32)


def dot_tn(left, right):
    return lax.dot_general(left, right, (((0,), (0,)), ((), ())), preferred_element_type=F32)


def sigmoid(v):
    return 0.5 * jnp.tanh(0.5 * v) + 0.5


def softplus(v):
    return jnp.maximum(v, 0.0) + jnp.log1p(jnp.exp(-jnp.abs(v)))


def iota2(shape, axis):
    return lax.broadcasted_iota(jnp.int32, shape, axis)


def column(values, index):
    return values[:, index : index + 1]


def spread(values, pair, low_half):
    return jnp.where(low_half, column(values, 2 * pair), column(values, 2 * pair + 1))


def convolve(ext_ref, taps_ref, bias_ref, masks, at):
    rows = masks.shape[0]
    cols = pl.ds(at, LANES)
    total = bias_ref[:, cols] + taps_ref[3:4, cols] * ext_ref[HALO : HALO + rows, cols]
    for back in range(1, 4):
        shifted = ext_ref[HALO - back : HALO - back + rows, cols]
        total = total + taps_ref[3 - back : 4 - back, cols] * shifted * column(masks, back - 1)
    return total


def forward_kernel(
    sizes,
    h_ref, masks_ref, segr_ref, w_ref, wout_ref, taps_ref, cbias_ref, gin_ref, ggate_ref,
    head_ref, skip_ref,
    next_ref, normed_ref, proj_ref, y_ref, gated_ref, states_ref,
    ext, xs, state,
):
    inner, xbc, nstate, pairs = sizes
    rows = h_ref.shape[0]

    @pl.when(pl.program_id(0) == 0)
    def _():
        state[...] = jnp.zeros_like(state)
        ext[0:HALO, :] = jnp.zeros((HALO, xbc), F32)

    hidden = h_ref[...].astype(F32)
    scale = lax.rsqrt(jnp.mean(hidden * hidden, axis=-1, keepdims=True) + EPSILON)
    normed_ref[...] = (hidden * scale * gin_ref[...]).astype(BF16)
    proj_ref[...] = dot_nn(normed_ref[...], w_ref[...])
    masks = masks_ref[...]
    ext[HALO : HALO + rows, :] = proj_ref[:, inner : inner + xbc]
    for at in range(0, xbc, LANES):
        v = convolve(ext, taps_ref, cbias_ref, masks, at)
        xs[:, at : at + LANES] = v * sigmoid(v)
    ext[0:HALO, :] = ext[rows : rows + HALO, :]

    low_half = iota2((CHUNK, LANES), 1) < LANES // 2
    low_row = iota2((1, LANES), 1) < LANES // 2
    t_at, s_at = iota2((CHUNK, CHUNK), 0), iota2((CHUNK, CHUNK), 1)
    tri = (t_at >= s_at).astype(F32)

    @pl.loop(0, rows // CHUNK)
    def _(c):
        span = pl.ds(pl.multiple_of(c * CHUNK, CHUNK), CHUNK)
        mk = masks_ref[span, :]
        dt = softplus(proj_ref[span, inner + xbc : inner + xbc + LANES] + head_ref[0:1, :])
        cum = dot_nn(tri, -head_ref[1:2, :] * dt, HIGHEST)
        cum_t, dt_t = cum.T, dt.T
        segr = segr_ref[c]
        bias = jnp.where((t_at >= s_at) & (column(mk, 8) == segr), 0.0, -1e30)
        b_f = xs[span, inner : inner + nstate]
        c_b = xs[span, inner + nstate : inner + 2 * nstate].astype(BF16)
        both = dot_nt(c_b, b_f.astype(BF16))
        b_t = b_f.T.astype(BF16)
        last = cum[CHUNK - 1 : CHUNK, :]
        from_state = jnp.exp(cum) * column(mk, 3)
        to_state = jnp.exp(last - cum) * column(mk, 4) * dt
        keep = jnp.exp(last) * mk[CHUNK - 1 : CHUNK, 3:4]
        for pair in range(pairs):
            cols = pl.ds(pair * LANES, LANES)
            x = xs[span, cols]
            x_b = x.astype(BF16)
            parts = []
            for head in (2 * pair, 2 * pair + 1):
                decay = jnp.exp(column(cum, head) - cum_t[head : head + 1, :] + bias)
                mix = decay * both * dt_t[head : head + 1, :]
                parts.append(dot_nn(mix.astype(BF16), x_b))
            inside = jnp.where(low_half, parts[0], parts[1])
            old = state[:, cols]
            states_ref[c, :, cols] = old
            outside = dot_nn(c_b, old.astype(BF16)) * spread(from_state, pair, low_half)
            fresh = dot_nn(b_t, (x * spread(to_state, pair, low_half)).astype(BF16))
            state[:, cols] = old * spread(keep, pair, low_row) + fresh
            y_ref[span, cols] = inside + outside + skip_ref[:, cols] * x

    total = jnp.zeros((rows, LANES), F32)
    for at in range(0, inner, LANES):
        z = proj_ref[:, at : at + LANES]
        g = y_ref[:, at : at + LANES] * (z * sigmoid(z))
        xs[:, at : at + LANES] = g
        total = total + g * g
    scale = lax.rsqrt(jnp.sum(total, axis=-1, keepdims=True) / inner + EPSILON)
    for at in range(0, inner, LANES):
        g = xs[:, at : at + LANES] * scale * ggate_ref[:, at : at + LANES]
        gated_ref[:, at : at + LANES] = g.astype(BF16)
    out = h_ref[...].astype(F32) + dot_nn(gated_ref[...], wout_ref[...])
    next_ref[...] = out.astype(next_ref.dtype)


def backward_kernel(
    sizes,
    dh_ref, h_ref, masks_ref, segr_ref, proj_ref, before_ref, y_ref, states_ref,
    w_ref, wout_ref, taps_ref, cbias_ref, gin_ref, ggate_ref, head_ref, skip_ref, fold_ref,
    dnext_ref, dproj_ref, sg_gate, sg_conv, sg_in, sg_skip, sg_head,
    ext, xs, conv, dy, dxs, dstate, rowsc, flat,
):
    inner, xbc, nstate, pairs = sizes
    rows = h_ref.shape[0]
    step = pl.program_id(0)

    @pl.when(step == 0)
    def _():
        dstate[...] = jnp.zeros_like(dstate)
        rowsc[...] = jnp.zeros_like(rowsc)
        flat[...] = jnp.zeros_like(flat)
        dxs[rows : rows + HALO, :] = jnp.zeros((HALO, xbc), F32)
        for ref in (sg_gate, sg_conv, sg_in, sg_skip, sg_head):
            ref[...] = jnp.zeros_like(ref)

    dh = dh_ref[...].astype(F32)
    dy[...] = dot_nt(dh.astype(BF16), wout_ref[...])

    squares = jnp.zeros((rows, LANES), F32)
    cross = jnp.zeros((rows, LANES), F32)
    for at in range(0, inner, LANES):
        cols = pl.ds(at, LANES)
        z = proj_ref[:, cols]
        g = y_ref[:, cols] * (z * sigmoid(z))
        squares = squares + g * g
        cross = cross + g * (dy[:, cols] * ggate_ref[:, cols])
    scale = lax.rsqrt(jnp.sum(squares, axis=-1, keepdims=True) / inner + EPSILON)
    mean = scale * jnp.sum(cross, axis=-1, keepdims=True) / inner
    for at in range(0, inner, LANES):
        cols = pl.ds(at, LANES)
        z = proj_ref[:, cols]
        sig = sigmoid(z)
        gate = z * sig
        y = y_ref[:, cols]
        m = y * gate * scale
        dgated = dy[:, cols]
        sg_gate[0:1, cols] += jnp.sum(m * dgated, axis=0, keepdims=True)
        dg = scale * (dgated * ggate_ref[:, cols] - m * mean)
        dproj_ref[:, cols] = (dg * y * (sig * (1.0 + z * (1.0 - sig)))).astype(BF16)
        dy[:, cols] = dg * gate

    masks = masks_ref[...]
    ext[0:HALO, :] = before_ref[:, inner : inner + xbc]
    ext[HALO : HALO + rows, :] = proj_ref[:, inner : inner + xbc]
    for at in range(0, xbc, LANES):
        v = convolve(ext, taps_ref, cbias_ref, masks, at)
        conv[:, at : at + LANES] = v
        xs[:, at : at + LANES] = v * sigmoid(v)

    low_half = iota2((CHUNK, LANES), 1) < LANES // 2
    low_row = iota2((1, LANES), 1) < LANES // 2
    lane = iota2((CHUNK, LANES), 1)
    s_at, t_at = iota2((CHUNK, CHUNK), 0), iota2((CHUNK, CHUNK), 1)
    tri = (s_at >= t_at).astype(F32)
    tri_t = (s_at <= t_at).astype(F32)
    last_row = iota2((CHUNK, LANES), 0) == CHUNK - 1
    chunks = rows // CHUNK

    @pl.loop(0, chunks)
    def _(back):
        c = chunks - 1 - back
        span = pl.ds(pl.multiple_of(c * CHUNK, CHUNK), CHUNK)
        mk = masks_ref[span, :]
        raw = proj_ref[span, inner + xbc : inner + xbc + LANES] + head_ref[0:1, :]
        dt = softplus(raw)
        speed = head_ref[1:2, :]
        cum = dot_nn(tri, -speed * dt, HIGHEST)
        cum_t = cum.T
        segr = segr_ref[c]
        bias = jnp.where((s_at <= t_at) & (column(mk, 8) == segr), 0.0, -1e30)
        b_b = xs[span, inner : inner + nstate].astype(BF16)
        c_f = xs[span, inner + nstate : inner + 2 * nstate]
        c_b = c_f.astype(BF16)
        c_t = c_f.T.astype(BF16)
        both = dot_nt(b_b, c_b)
        last = cum[CHUNK - 1 : CHUNK, :]
        from_state = jnp.exp(cum) * column(mk, 3)
        to_bare = jnp.exp(last - cum) * column(mk, 4)
        to_state = to_bare * dt
        keep = jnp.exp(last) * mk[CHUNK - 1 : CHUNK, 3:4]
        dboth = jnp.zeros((CHUNK, CHUNK), F32)
        db = jnp.zeros((CHUNK, nstate), F32)
        dc = jnp.zeros((CHUNK, nstate), F32)
        ddt = jnp.zeros((CHUNK, LANES), F32)
        dto = jnp.zeros((CHUNK, LANES), F32)
        dfrom = jnp.zeros((CHUNK, LANES), F32)
        for pair in range(pairs):
            cols = pl.ds(pair * LANES, LANES)
            x = xs[span, cols]
            d = dy[span, cols]
            d_b = d.astype(BF16)
            old = states_ref[c, :, cols]
            old_b = old.astype(BF16)
            dnew = dstate[:, cols]
            dnew_b = dnew.astype(BF16)
            weight = spread(to_state, pair, low_half)
            scaled = d * spread(from_state, pair, low_half)
            scaled_b = scaled.astype(BF16)
            reach = scaled * dot_nn(c_b, old_b)
            pull = dot_nn(b_b, dnew_b)
            dc = dc + dot_nt(scaled_b, old_b)
            db = db + dot_nt((x * weight).astype(BF16), dnew_b)
            flat[0:1, cols] = jnp.sum(dnew * old, axis=0, keepdims=True)
            dstate[:, cols] = dot_nn(c_t, scaled_b) + dnew * spread(keep, pair, low_row)
            gain = x * pull
            parts = []
            for head in (2 * pair, 2 * pair + 1):
                mine = low_half if head % 2 == 0 else jnp.logical_not(low_half)
                dt_col = column(dt, head)
                x_m = jnp.where(mine, x, 0.0).astype(BF16)
                decay = jnp.exp(cum_t[head : head + 1, :] - column(cum, head) + bias)
                prod = dot_nt(x_m, d_b)
                mix = decay * both
                parts.append(dot_nn(mix.astype(BF16), d_b))
                inner_prod = mix * prod
                dboth = dboth + decay * prod * dt_col
                rowsc[head : head + 1, :] = jnp.sum(inner_prod * dt_col, axis=0, keepdims=True)
                here = lane == head
                ddt = jnp.where(here, jnp.sum(inner_prod, axis=1, keepdims=True), ddt)
                dto = jnp.where(
                    here, jnp.sum(jnp.where(mine, gain, 0.0), axis=1, keepdims=True), dto
                )
                dfrom = jnp.where(
                    here, jnp.sum(jnp.where(mine, reach, 0.0), axis=1, keepdims=True), dfrom
                )
            inside = jnp.where(low_half, parts[0], parts[1]) * spread(dt, pair, low_half)
            dxs[span, cols] = inside + weight * pull + skip_ref[:, cols] * d
            sg_skip[0:1, cols] += jnp.sum(d * x, axis=0, keepdims=True)
        dxs[span, inner : inner + nstate] = db + dot_nn(dboth.astype(BF16), c_b)
        dxs[span, inner + nstate : inner + 2 * nstate] = dc + dot_nn(dboth.T.astype(BF16), b_b)
        moved = dto * to_state
        dlast = dot_nn(flat[...], fold_ref[...], HIGHEST)[0:1, :] * keep
        dlast = dlast + jnp.sum(moved, axis=0, keepdims=True)
        dcum = rowsc[...].T + dfrom - dt * ddt - moved
        dcum = dcum + jnp.where(last_row, dlast, 0.0)
        drate = dot_nn(tri_t, dcum, HIGHEST)
        dtotal = ddt + dto * to_bare - speed * drate
        draw = dtotal * sigmoid(raw)
        dproj_ref[span, inner + xbc : inner + xbc + LANES] = draw.astype(BF16)
        sg_head[0:1, :] += jnp.sum(draw, axis=0, keepdims=True)
        sg_head[1:2, :] += jnp.sum(-speed * dt * drate, axis=0, keepdims=True)

    for at in range(0, xbc, LANES):
        cols = pl.ds(at, LANES)
        v = conv[:, cols]
        sig = sigmoid(v)
        dconv = dxs[0:rows, cols] * (sig * (1.0 + v * (1.0 - sig)))
        dxs[0:rows, cols] = dconv
        sg_conv[4:5, cols] += jnp.sum(dconv, axis=0, keepdims=True)
        sg_conv[3:4, cols] += jnp.sum(dconv * ext[HALO : HALO + rows, cols], axis=0, keepdims=True)
        total = dconv * taps_ref[3:4, cols]
        for back in range(1, 4):
            shifted = ext[HALO - back : HALO - back + rows, cols] * column(masks, back - 1)
            sg_conv[3 - back : 4 - back, cols] += jnp.sum(dconv * shifted, axis=0, keepdims=True)
            later = dxs[back : back + rows, cols] * column(masks, 4 + back)
            total = total + later * taps_ref[3 - back : 4 - back, cols]
        dproj_ref[:, inner + at : inner + at + LANES] = total.astype(BF16)
    dxs[rows : rows + HALO, :] = dxs[0:HALO, :]

    dnormed = dot_nt(dproj_ref[...], w_ref[...])
    hidden = h_ref[...].astype(F32)
    scale = lax.rsqrt(jnp.mean(hidden * hidden, axis=-1, keepdims=True) + EPSILON)
    m = hidden * scale
    sg_in[0:1, :] += jnp.sum(m * dnormed, axis=0, keepdims=True)
    dm = dnormed * gin_ref[...]
    dnext_ref[...] = dh_ref[...].astype(F32) + scale * (
        dm - m * jnp.mean(dm * m, axis=-1, keepdims=True)
    )


def whole(array):
    return pl.BlockSpec(array.shape, lambda i: (0,) * array.ndim)


def dims(hidden, weights):
    length, width = hidden.shape
    inner = weights["w_out"].shape[0]
    xbc = weights["taps"].shape[1]
    nstate = (xbc - inner) // 2
    return length, width, inner, xbc, nstate, inner // LANES


def run_forward(hidden, masks, segr, weights, heads, skip, out_type):
    length, width, inner, xbc, nstate, pairs = dims(hidden, weights)
    packed = inner + xbc + LANES
    steps = length // ROWS
    per = ROWS // CHUNK

    def rows(cols):
        return pl.BlockSpec((ROWS, cols), lambda i: (i, 0))

    fixed = (weights["w"], weights["w_out"], weights["taps"], weights["cbias"], weights["g_in"],
             weights["g_gate"], heads, skip)
    return pl.pallas_call(
        functools.partial(forward_kernel, (inner, xbc, nstate, pairs)),
        grid=(steps,),
        in_specs=[rows(width), rows(masks.shape[1]),
                  pl.BlockSpec((per, 1, CHUNK), lambda i: (i, 0, 0))] + [whole(a) for a in fixed],
        out_specs=[rows(width), rows(width), rows(packed), rows(inner), rows(inner),
                   pl.BlockSpec((per, nstate, inner), lambda i: (i, 0, 0))],
        out_shape=[
            jax.ShapeDtypeStruct((length, width), out_type),
            jax.ShapeDtypeStruct((length, width), BF16),
            jax.ShapeDtypeStruct((length, packed), F32),
            jax.ShapeDtypeStruct((length, inner), F32),
            jax.ShapeDtypeStruct((length, inner), BF16),
            jax.ShapeDtypeStruct((length // CHUNK, nstate, inner), F32),
        ],
        scratch_shapes=[
            pltpu.VMEM((ROWS + HALO, xbc), F32),
            pltpu.VMEM((ROWS, xbc), F32),
            pltpu.VMEM((nstate, inner), F32),
        ],
        compiler_params=pltpu.CompilerParams(vmem_limit_bytes=VMEM_BYTES),
        cost_estimate=pl.CostEstimate(
            flops=60_000_000_000, bytes_accessed=60_000_000, transcendentals=6_000_000),
        name="layer_forward",
    )(hidden, masks, segr, *fixed)


def run_backward(grad, hidden, masks, segr, saved, weights, heads, skip, fold):
    length, width, inner, xbc, nstate, pairs = dims(hidden, weights)
    packed = inner + xbc + LANES
    steps = length // ROWS
    per = ROWS // CHUNK
    proj, y, states = saved

    def rows(cols):
        return pl.BlockSpec((ROWS, cols), lambda i: (steps - 1 - i, 0))

    def before(i):
        return (jnp.maximum((steps - 1 - i) * (ROWS // HALO) - 1, 0), 0)

    fixed = (weights["w"], weights["w_out"], weights["taps"], weights["cbias"], weights["g_in"],
             weights["g_gate"], heads, skip, fold)
    sums = [(8, inner), (8, xbc), (8, width), (8, inner), (8, LANES)]
    return pl.pallas_call(
        functools.partial(backward_kernel, (inner, xbc, nstate, pairs)),
        grid=(steps,),
        in_specs=[rows(width), rows(width), rows(masks.shape[1]),
                  pl.BlockSpec((per, 1, CHUNK), lambda i: (steps - 1 - i, 0, 0)),
                  rows(packed), pl.BlockSpec((HALO, packed), before), rows(inner),
                  pl.BlockSpec((per, nstate, inner), lambda i: (steps - 1 - i, 0, 0))]
        + [pl.BlockSpec(a.shape, lambda i: (0, 0), pipeline_mode=pl.Buffered(1)) for a in fixed],
        out_specs=[rows(width), rows(packed)] + [pl.BlockSpec(s, lambda i: (0, 0)) for s in sums],
        out_shape=[
            jax.ShapeDtypeStruct((length, width), F32),
            jax.ShapeDtypeStruct((length, packed), BF16),
        ] + [jax.ShapeDtypeStruct(s, F32) for s in sums],
        scratch_shapes=[
            pltpu.VMEM((ROWS + HALO, xbc), F32),
            pltpu.VMEM((ROWS, xbc), F32),
            pltpu.VMEM((ROWS, xbc), F32),
            pltpu.VMEM((ROWS, inner), F32),
            pltpu.VMEM((ROWS + HALO, xbc), F32),
            pltpu.VMEM((nstate, inner), F32),
            pltpu.VMEM((LANES, CHUNK), F32),
            pltpu.VMEM((8, inner), F32),
        ],
        compiler_params=pltpu.CompilerParams(vmem_limit_bytes=VMEM_BYTES),
        cost_estimate=pl.CostEstimate(
            flops=120_000_000_000, bytes_accessed=80_000_000, transcendentals=6_000_000),
        name="layer_backward",
    )(grad, hidden, masks, segr, proj, proj, y, states, *fixed)


def token_masks(segment):
    length = segment.shape[0]
    blocks = segment.reshape(length // CHUNK, CHUNK)
    keeps, laters = [], []
    for back in range(1, 4):
        same = (segment[back:] == segment[:-back]).astype(F32)
        keeps.append(jnp.pad(same, (back, 0)))
        laters.append(jnp.pad(same, (0, back)))
    before = jnp.concatenate([jnp.full((1,), -1, jnp.int32), blocks[:-1, -1]])
    carried = (blocks == before[:, None]).astype(F32).reshape(length)
    lasting = (blocks == blocks[:, -1:]).astype(F32).reshape(length)
    number = segment.astype(F32)
    columns = keeps + [carried, lasting] + laters + [number]
    masks = jnp.pad(jnp.stack(columns, axis=1), ((0, 0), (0, 16 - len(columns))))
    return masks, number.reshape(length // CHUNK, 1, CHUNK)


def as_columns(flat, rows):
    columns = -(-flat.shape[-1] // rows)
    fill = rows * columns - flat.shape[-1]
    flat = jnp.pad(flat, [(0, 0)] * (flat.ndim - 1) + [(0, fill)])
    return flat.reshape(*flat.shape[:-1], rows, columns)


def pack_layer(w_in, w_dt, conv_w, conv_b, norm_in, norm_gate):
    rows = w_in.shape[0]
    small = as_columns(jnp.concatenate([conv_w.reshape(-1), conv_b, norm_in, norm_gate]), rows)
    unused = LANES - w_dt.shape[1] - small.shape[1]
    return jnp.concatenate([w_in, w_dt, small, jnp.zeros((rows, unused), BF16)], axis=1)


def unpack_layer(wide, w_out, start, rows, taps, chan, gain_in):
    group = wide.shape[0] // rows
    gain_gate = w_out.shape[0] // group
    cut = taps * chan
    count = cut + chan + gain_in + gain_gate
    width = -(-count // rows)
    small = wide[:, start : start + width].reshape(group, rows * width).astype(F32)
    conv = small[:, :cut].reshape(group, taps, chan).transpose(1, 0, 2).reshape(taps, -1)
    return {
        "w": wide,
        "w_out": w_out,
        "taps": jnp.pad(conv, ((0, 8 - taps), (0, 0))),
        "cbias": small[:, cut : cut + chan].reshape(1, -1),
        "g_in": small[:, cut + chan : cut + chan + gain_in].reshape(1, -1),
        "g_gate": small[:, cut + chan + gain_in : count].reshape(1, -1),
    }


def gather(array):
    return lax.all_gather(array, "fsdp", axis=0, tiled=True)


def scatter(array):
    return lax.psum_scatter(array, "fsdp", scatter_dimension=0, tiled=True)


def shards(
    tokens, segments, w_in, w_dt, w_out, conv_w, conv_b, norm_in, norm_gate,
    dt_bias, a_log, d_skip, cotangent,
):
    layers, heads = dt_bias.shape
    group = lax.axis_size("fsdp")
    masks, segr = token_masks(segments[0])
    headdim = w_out.shape[1] * group // heads
    inner = heads * headdim
    fold = (jnp.arange(inner)[:, None] // headdim == jnp.arange(LANES)[None, :]).astype(F32)
    rows, columns = w_in.shape[1:]
    taps, chan = conv_w.shape[1:]
    gain = norm_in.shape[1]
    used = columns + heads
    weights, head_rows, skips = [], [], []
    for l in range(layers):
        packed = pack_layer(w_in[l], w_dt[l], conv_w[l], conv_b[l], norm_in[l], norm_gate[l])
        weights.append(unpack_layer(
            gather(packed), gather(w_out[l]), used, rows, taps, chan, gain))
        both = jnp.stack([dt_bias[l], jnp.exp(a_log[l])])
        head_rows.append(jnp.pad(both, ((0, 6), (0, LANES - heads))))
        skips.append(jnp.repeat(d_skip[l], headdim)[None, :])
    hiddens, saved = [tokens[0]], []
    for l in range(layers):
        out_type = BF16 if l == layers - 1 else F32
        following, normed, proj, y, gated, states = run_forward(
            hiddens[l], masks, segr, weights[l], head_rows[l], skips[l], out_type)
        hiddens.append(following)
        saved.append((normed, gated, (proj, y, states)))
    grad = cotangent[0]
    wides, outs = [None] * layers, [None] * layers
    pending = []
    for l in reversed(range(layers)):
        normed, gated, kept = saved[l]
        out_grad = dot_tn(gated, grad.astype(BF16)).astype(BF16)
        out_grad, grad = lax.optimization_barrier((out_grad, grad))
        out_part = scatter(out_grad)
        if pending:
            part, grad = lax.optimization_barrier((pending[0], grad))
            outs[l + 1] = lax.psum(part, "rep")
        grad, dproj, s_gate, s_conv, s_in, s_skip, s_head = run_backward(
            grad, hiddens[l], masks, segr, kept, weights[l], head_rows[l], skips[l], fold)
        per_head = jnp.concatenate([
            s_head[0, :heads], s_head[1, :heads], s_skip[0].reshape(heads, headdim).sum(-1)])
        small = jnp.concatenate([
            s_conv[:5].reshape(5, group, -1).transpose(1, 0, 2).reshape(group, -1),
            s_in[0].reshape(group, -1),
            s_gate[0].reshape(group, -1),
            jnp.broadcast_to(per_head, (group, per_head.size)),
        ], axis=1)
        block = as_columns(small, rows)
        block = block.reshape(group * rows, block.shape[-1]).astype(BF16)
        wide = dot_tn(normed, dproj).astype(BF16)
        wide = lax.dynamic_update_slice(wide, block, (0, used))
        wides[l] = scatter(wide)
        outs[l] = out_part
        pending = [out_part]
    *wides, outs[0] = lax.psum((*wides, outs[0]), "rep")
    wide = jnp.stack(wides).astype(F32)
    count = small.shape[1]
    vectors = wide[:, :, used : used + block.shape[1]].reshape(layers, -1)[:, :count]
    ends = [taps * chan, (taps + 1) * chan, (taps + 1) * chan + gain, count - 3 * heads]
    per_head = vectors[:, ends[3] :].reshape(layers, 3, heads)
    return (
        hiddens[-1][None],
        grad[None],
        wide[:, :, :columns],
        wide[:, :, columns:used],
        jnp.stack(outs).astype(F32),
        vectors[:, : ends[0]].reshape(layers, taps, chan),
        vectors[:, ends[0] : ends[1]],
        vectors[:, ends[1] : ends[2]],
        vectors[:, ends[2] : ends[3]],
        per_head[:, 0],
        per_head[:, 1],
        per_head[:, 2],
    )


def solution(mesh):
    sharded = P(None, "fsdp", None)
    tokens = P(("rep", "fsdp"), None, None)
    narrow = P(None, "fsdp")
    return jax.shard_map(
        shards,
        mesh=mesh,
        in_specs=(
            tokens, P(("rep", "fsdp"), None), sharded, sharded, sharded, P(None, None, "fsdp"),
            narrow, narrow, narrow, P(), P(), P(), tokens,
        ),
        out_specs=(
            tokens, tokens, sharded, sharded, sharded, P(None, None, "fsdp"),
            narrow, narrow, narrow, P(), P(), P(),
        ),
        check_vma=False,
    )
```
